32 devices in a mesh: dp: 2 (over core), seq: 16 (over z, y, x).
Axes of the slice: x: 2, y: 2, z: 4, core: 2. Of those that a mesh axis runs over, the one named last changes fastest.
Arguments:
- queries: bfloat16 [2, 2048, 512], P('dp', 'seq'), may hold values from -6 to 6
- keys: bfloat16 [2, 2048, 512], P('dp', 'seq'), may hold values from -6 to 6
- values: bfloat16 [2, 2048, 512], P('dp', 'seq'), may hold values from -12 to 12
- residual: bfloat16 [2, 2048, 1024], P('dp', 'seq'), may hold values from -3 to 3
- out_proj: bfloat16 [512, 1024], replicated, may hold values from -0.25 to 0.25
- conv_in: bfloat16 [1024, 2048], P(None, 'seq'), may hold values from -0.1875 to 0.1875
- conv_out: bfloat16 [1024, 1024], replicated, may hold values from -0.1875 to 0.1875
- depth_kernel: bfloat16 [31, 1024], replicated, may hold values from -1 to 1
- norm_gain: float32 [1024], replicated, may hold values from 0.25 to 1.75
- cotangent: bfloat16 [2, 2048, 1024], P('dp', 'seq'), may hold values from -6 to 6
Outputs:
- layer_out: bfloat16 [2, 2048, 1024], P('dp', 'seq')
- grad_mid: bfloat16 [2, 2048, 1024], P('dp', 'seq')
- grad_out_proj: float32 [512, 1024], P('seq')
- grad_kernel: float32 [31, 1024], replicated
The draws below stay inside these ranges and needn't reach their ends.
All inputs are finite; a program needn't handle non-finite values.
Results may differ from the reference program's by a relative error of at most 0.015.
Values may be sent and summed in bfloat16 or wider, within the bound.
A program may use at most 128 MiB of HBM per device.

```python
import math
import jax
import jax.numpy as jnp
from jax import lax

D = 1024
HEADS = 8
DH = 64
KW = 31
BATCH = 2
LENGTH = 2048


def paired_draw(key):
    base = jax.random.fold_in(key, 7)
    first, second = jax.random.split(base, 2)
    shape = (BATCH, LENGTH, HEADS * DH)
    query_draw = jnp.clip(1.5 * jax.random.normal(first, shape, jnp.float32), -6.0, 6.0)
    key_draw = jnp.clip(1.5 * jax.random.normal(second, shape, jnp.float32), -6.0, 6.0)
    return (query_draw, key_draw)


def draw_queries(key, part):
    return paired_draw(key)[0].astype(jnp.bfloat16)


def draw_keys(key, part):
    return paired_draw(key)[1].astype(jnp.bfloat16)


def block_levels(stream_key, dims, shards, least, high):
    gain = 1.0
    for position, shards_of in shards:
        steps = jax.random.uniform(jax.random.fold_in(jax.random.fold_in(stream_key, 6), position), (shards_of,), jnp.float32, least / len(shards), high / len(shards))
        gain = gain * jnp.repeat(jnp.exp(steps), dims[position] // shards_of).reshape((-1,) + (1,) * (len(dims) - 1 - position))
    return gain


def centred(stream_key, dims, spread, most, shards=(), held_as=jnp.bfloat16):
    values = jax.random.normal(stream_key, dims, jnp.float32) * spread
    if len(shards) > 0:
        values = block_levels(stream_key, dims, shards, -0.22, 0.18) * values
    return jnp.clip(values, min=-most, max=most).astype(held_as)


def setup_inputs(seed: int = 0) -> dict:
    key_list = jax.random.split(jax.random.key(seed), 11)
    queries = draw_queries(jax.random.fold_in(key_list[10], 71), 0)
    keys = draw_keys(jax.random.fold_in(key_list[10], 71), 0)
    values = centred(key_list[2], (BATCH, LENGTH, HEADS * DH), 2.0, 12.0, ((0, 2), (1, 16)))
    residual = centred(key_list[3], (BATCH, LENGTH, D), 0.5, 3.0, ((0, 2), (1, 16)))
    out_proj = centred(key_list[4], (HEADS * DH, D), (HEADS * DH) ** -0.5, 0.25)
    conv_in = centred(key_list[5], (D, 2 * D), D ** -0.5, 0.1875, ((1, 16),))
    conv_out = centred(key_list[6], (D, D), D ** -0.5, 0.1875)
    depth_kernel = centred(key_list[7], (KW, D), KW ** -0.5, 1.0)
    norm_gain = jnp.clip(1.0 + 0.15 * jax.random.normal(key_list[8], (D,), jnp.float32), 0.25, 1.75)
    cotangent = centred(key_list[9], (BATCH, LENGTH, D), 1.0, 6.0, ((0, 2), (1, 16)))
    return dict(queries=queries, keys=keys, values=values, residual=residual, out_proj=out_proj, conv_in=conv_in, conv_out=conv_out, depth_kernel=depth_kernel, norm_gain=norm_gain, cotangent=cotangent)


norm_epsilon = 1e-05

def attend_one(triple):
    query, key_rows, value_rows = triple
    length = query.shape[0]
    block = math.gcd(length, 512)
    query_blocks = query.reshape(length // block, block, query.shape[1])

    def one_block(query_block):
        scores = lax.dot_general(query_block, key_rows, (((1,), (1,)), ((), ())), preferred_element_type=jnp.float32) * DH ** (-0.5)
        highest = lax.optimization_barrier(jnp.max(scores, axis=1, keepdims=True))
        expo = jnp.exp(scores - highest)
        total = lax.optimization_barrier(jnp.sum(expo, axis=1, keepdims=True))
        weights = expo.astype(jnp.bfloat16)
        mixed = jnp.dot(weights, value_rows, preferred_element_type=jnp.float32)
        return (mixed / total).astype(jnp.bfloat16)
    return lax.map(one_block, query_blocks).reshape(length, query.shape[1])

def layer_norm(mid):
    wide = mid.astype(jnp.float32)
    centered = wide - lax.optimization_barrier(jnp.mean(wide, axis=-1, keepdims=True))
    rscale = lax.rsqrt(lax.optimization_barrier(jnp.mean(centered * centered, axis=-1, keepdims=True)) + norm_epsilon)
    return (centered * rscale, rscale)

def depth_forward(padded, kernel, rows):
    total = jnp.zeros((padded.shape[0], rows, padded.shape[2]), jnp.float32)
    for offset in range(KW):
        total = total + kernel[offset].astype(jnp.float32) * padded[:, offset:offset + rows].astype(jnp.float32)
    return total

def depth_backward(padded, kernel, rows):
    total = jnp.zeros((padded.shape[0], rows, padded.shape[2]), jnp.float32)
    reach = (KW - 1) // 2
    for offset in range(KW):
        begin = 2 * reach - offset
        total = total + kernel[offset].astype(jnp.float32) * padded[:, begin:begin + rows].astype(jnp.float32)
    return total

def kernel_terms(padded, grad_conv, rows):
    terms = []
    for offset in range(KW):
        product = padded[:, offset:offset + rows].astype(jnp.float32) * grad_conv.astype(jnp.float32)
        terms.append(lax.optimization_barrier(jnp.sum(product, axis=(0, 1))))
    return jnp.stack(terms, axis=0)

def reference(queries, keys, values, residual, out_proj, conv_in, conv_out, depth_kernel, norm_gain, cotangent):
    batch, length, width = queries.shape
    model = residual.shape[2]
    reach = (KW - 1) // 2

    def split_heads(array):
        return array.reshape(batch, length, HEADS, DH).transpose(0, 2, 1, 3).reshape(batch * HEADS, length, DH)
    heads_out = lax.map(attend_one, (split_heads(queries), split_heads(keys), split_heads(values)))
    attended = heads_out.reshape(batch, HEADS, length, DH).transpose(0, 2, 1, 3).reshape(batch * length, width)
    flat_resid = residual.reshape(batch * length, model).astype(jnp.float32)
    mid = (flat_resid + jnp.dot(attended, out_proj, preferred_element_type=jnp.float32)).astype(jnp.bfloat16)
    hat, rscale = layer_norm(mid)
    normed = (hat * norm_gain).astype(jnp.bfloat16)
    proj = jnp.dot(normed, conv_in, preferred_element_type=jnp.float32)
    value_half = proj[:, :model]
    gate_half = jax.nn.sigmoid(proj[:, model:])
    gated = (value_half * gate_half).astype(jnp.bfloat16).reshape(batch, length, model)
    padded = jnp.pad(gated, ((0, 0), (reach, reach), (0, 0)))
    conv = depth_forward(padded, depth_kernel, length)
    act = (conv * jax.nn.sigmoid(conv)).astype(jnp.bfloat16).reshape(batch * length, model)
    layer_out = (mid.astype(jnp.float32) + jnp.dot(act, conv_out, preferred_element_type=jnp.float32)).astype(jnp.bfloat16)
    flat_cot = cotangent.reshape(batch * length, model)
    grad_act = lax.dot_general(flat_cot, conv_out, (((1,), (1,)), ((), ())), preferred_element_type=jnp.float32)
    sig_conv = jax.nn.sigmoid(conv).reshape(batch * length, model)
    conv_flat = conv.reshape(batch * length, model)
    grad_conv = (grad_act * sig_conv * (1.0 + conv_flat * (1.0 - sig_conv))).astype(jnp.bfloat16).reshape(batch, length, model)
    grad_padded = jnp.pad(grad_conv, ((0, 0), (reach, reach), (0, 0)))
    grad_gated = depth_backward(grad_padded, depth_kernel, length).reshape(batch * length, model)
    grad_kernel = kernel_terms(padded, grad_conv, length)
    grad_proj = jnp.concatenate([grad_gated * gate_half, grad_gated * value_half * gate_half * (1.0 - gate_half)], axis=1).astype(jnp.bfloat16)
    grad_normed = lax.dot_general(grad_proj, conv_in, (((1,), (1,)), ((), ())), preferred_element_type=jnp.float32)
    scaled = grad_normed * norm_gain
    inner = scaled - lax.optimization_barrier(jnp.mean(scaled, axis=1, keepdims=True)) - hat * lax.optimization_barrier(jnp.mean(scaled * hat, axis=1, keepdims=True))
    grad_mid = (flat_cot.astype(jnp.float32) + rscale * inner).astype(jnp.bfloat16)
    grad_out_proj = lax.dot_general(attended, grad_mid, (((0,), (0,)), ((), ())), preferred_element_type=jnp.float32)
    return (layer_out.reshape(batch, length, model), grad_mid.reshape(batch, length, model), grad_out_proj, grad_kernel)
```

```python
import functools

import jax
import jax.numpy as jnp
from jax import lax
from jax.experimental import pallas as pl
from jax.experimental.pallas import tpu as pltpu
from jax.sharding import PartitionSpec as P

HEADS = 8
DH = 64
KW = 31
EPS = 1e-05
F32 = jnp.float32
BF16 = jnp.bfloat16
MESH = pl.DeviceIdType.MESH


def sigmoid(x):
    return 1.0 / (1.0 + jnp.exp(-x))


def toggled(me, r):
    out = me
    b = 1
    while b <= r:
        if r & b:
            out = out + b * (1 - 2 * ((me // b) % 2))
        b *= 2
    return out


def kernel(
    S, DPN,
    q_ref, k_ref, v_ref, res_ref, op_ref, ci_ref, co_ref, dk_ref, ng_ref, ct_ref,
    lo_ref, gm_ref, go_ref, gk_ref,
    kvs, kvr, qs, qr, ats, atr, wf,
    att_ref, mid_ref, val_ref, gate_ref, gact_ref, act_ref, gcb_ref, gp, cp, gproj_ref,
    halo_s, halo_r, dkf,
    gkl, gk1s, gk1r, gk2s, gk2r, gk3r,
    gods, godr, gos, gor, gofr,
    kv_ss, kv_rs, q_ss, q_rs, at_ss, at_rs, w_ss, w_rs, sb_ss, sb_rs,
    h_ss, h_rs, k1_ss, k1_rs, k2_ss, k2_rs, k3_ss, k3_rs,
    gd_ss, gd_rs, g_ss, g_rs, gf_ss, gf_rs,
):
    me = lax.axis_index("seq")
    dp = lax.axis_index("dp")
    rows, model = res_ref.shape
    group = S // HEADS
    part = rows // group
    cw = ci_ref.shape[1]
    bits = []
    b = S // 2
    while b >= 1:
        bits.append(b)
        b //= 2
    order_a = bits
    order_b = bits[:-2] + [bits[-1], bits[-2]]

    def rc(src, dst, ss, rs, seq_id, dp_id):
        return pltpu.make_async_remote_copy(
            src_ref=src, dst_ref=dst, send_sem=ss, recv_sem=rs,
            device_id=(dp_id, seq_id), device_id_type=MESH,
        )

    def peers(fn, n, mine):
        def step(i, c):
            fn(lax.rem(mine + i, n))
            return c
        lax.fori_loop(1, n, step, 0)

    barrier = pltpu.get_barrier_semaphore()

    def hello_seq(j):
        pl.semaphore_signal(barrier, inc=1, device_id=(dp, j), device_id_type=MESH)

    def hello_dp(j):
        pl.semaphore_signal(barrier, inc=1, device_id=(j, me), device_id_type=MESH)

    peers(hello_seq, S, me)
    peers(hello_dp, DPN, dp)

    zeros64 = jnp.zeros((part, DH), BF16)
    for h in range(HEADS):
        cols = slice(h * DH, (h + 1) * DH)
        kvs[h] = jnp.concatenate([k_ref[:, cols], v_ref[:, cols]], axis=1)
        for g in range(group):
            piece = q_ref[g * part:(g + 1) * part, cols] * jnp.asarray(DH ** -0.5, BF16)
            qs[h * group + g] = jnp.concatenate([piece, zeros64], axis=1)
    wf[me] = ci_ref[...]
    pl.semaphore_wait(barrier, S - 1 + DPN - 1)

    def kv_copy(j, src):
        return rc(kvs.at[j // group], kvr.at[src], kv_ss.at[j], kv_rs.at[src], j, dp)

    def q_copy(j, src):
        return rc(qs.at[j], qr.at[src], q_ss.at[j], q_rs.at[src], j, dp)

    def send_qkv(j):
        kv_copy(j, me).start()
        q_copy(j, me).start()

    peers(send_qkv, S, me)
    kvr[me] = kvs[me // group]
    qr[me] = qs[me]

    share = 2 if DPN % 2 == 0 else 1
    core = lax.rem(dp, share)
    sib = dp + 1 - 2 * core
    half = model // share
    sub = half // 2

    def w_copy(o, r, b):
        chunk = toggled(me, r)
        begin = pl.multiple_of(core * half + o * sub, sub)
        where = wf.at[chunk, pl.ds(begin, sub)]
        return rc(where, where, w_ss.at[o, r + b], w_rs.at[o, r + b], toggled(me, b), dp)

    def sib_copy(r):
        where = wf.at[toggled(me, r), pl.ds(pl.multiple_of(core * half, half), half)]
        return rc(where, where, sb_ss.at[r], sb_rs.at[r], me, sib)

    def sib_recv(r):
        where = wf.at[toggled(me, r), pl.ds(pl.multiple_of((1 - core) * half, half), half)]
        return rc(where, where, sb_ss.at[r], sb_rs.at[r], me, sib)

    def subsets(order, n):
        out = [0]
        for b in order[:n]:
            out = out + [r + b for r in out]
        return out

    def w_recv_wait(o, r, b):
        chunk = toggled(me, r + b)
        begin = pl.multiple_of(core * half + o * sub, sub)
        where = wf.at[chunk, pl.ds(begin, sub)]
        rc(where, where, w_ss.at[o, r + b], w_rs.at[o, r + b], toggled(me, b), dp).wait_recv()

    done = set()

    def gather_step(n):
        for o, order in enumerate((order_a, order_b)):
            if n > 0:
                for r in subsets(order, n - 1):
                    w_recv_wait(o, r, order[n - 1])
            if n < len(bits):
                for r in subsets(order, n):
                    w_copy(o, r, order[n]).start()
        if share == 2:
            both = set(subsets(order_a, n)) & set(subsets(order_b, n))
            for r in sorted(both - done - {0}):
                sib_copy(r).start()
                done.add(r)

    gather_step(0)

    def wait_qkv(j):
        kv_copy(j, j).wait_recv()
        q_copy(j, j).wait_recv()

    peers(wait_qkv, S, me)
    gather_step(1)

    owners = max(1, 256 // part)
    blocks = S // owners
    kv = kvr[...].reshape(S * rows, 2 * DH)

    def at_copy(j, src):
        return rc(ats.at[j], atr.at[src], at_ss.at[j], at_rs.at[src], j, dp)

    def attend(i, c):
        first = i * owners
        q = qr[pl.ds(first, owners)].reshape(owners * part, 2 * DH)
        s = lax.dot_general(q, kv, (((1,), (1,)), ((), ())), preferred_element_type=F32)
        top = jnp.max(s, axis=1, keepdims=True)
        e = jnp.exp(s - top)
        total = jnp.sum(e, axis=1, keepdims=True)
        mixed = jnp.dot(e.astype(BF16), kv, preferred_element_type=F32)
        out = (mixed / total).astype(BF16).reshape(owners, part, 2 * DH)
        ats[pl.ds(first, owners)] = out

        def send(n, c2):
            j = first + n

            @pl.when(j != me)
            def _():
                at_copy(j, me).start()
            return c2
        lax.fori_loop(0, owners, send, 0)
        return c

    lax.fori_loop(0, blocks // 2, attend, 0)
    gather_step(2)
    lax.fori_loop(blocks // 2, blocks, attend, 0)
    for n in range(3, len(bits)):
        gather_step(n)
    atr[me] = ats[me]
    dkf[0:KW] = dk_ref[...].astype(F32)

    ct = ct_ref[...]
    gact_ref[...] = lax.dot_general(
        ct, co_ref[...], (((1,), (1,)), ((), ())), preferred_element_type=F32
    )

    def wait_at(j):
        at_copy(j, j).wait_recv()

    peers(wait_at, S, me)
    for g in range(group):
        for h in range(0, HEADS, 2):
            left = atr[h * group + g][:, DH:]
            right = atr[(h + 1) * group + g][:, DH:]
            att_ref[g * part:(g + 1) * part, h * DH:(h + 2) * DH] = jnp.concatenate(
                [left, right], axis=1
            )
    mid = (
        res_ref[...].astype(F32)
        + jnp.dot(att_ref[...], op_ref[...], preferred_element_type=F32)
    ).astype(BF16)
    mid_ref[...] = mid
    wide = mid.astype(F32)
    centered = wide - jnp.mean(wide, axis=1, keepdims=True)
    rscale = lax.rsqrt(jnp.mean(centered * centered, axis=1, keepdims=True) + EPS)
    gain = ng_ref[...]
    normed = (centered * rscale * gain).astype(BF16)

    gather_step(len(bits))
    if share == 2:
        for r in range(1, S):
            sib_recv(r).wait_recv()

    per = max(1, 256 // cw)
    wide_cols = per * cw

    def weights(n):
        return jnp.concatenate([wf[n * per + i] for i in range(per)], axis=1)

    count = model // wide_cols
    for n in range(count):
        cols = slice(n * wide_cols, (n + 1) * wide_cols)
        value = jnp.dot(normed, weights(n), preferred_element_type=F32)
        gate = sigmoid(jnp.dot(normed, weights(count + n), preferred_element_type=F32))
        val_ref[:, cols] = value
        gate_ref[:, cols] = gate
        gated = (value * gate).astype(BF16)
        gp[16:16 + rows, cols] = gated.astype(F32)
        halo_s[0, :, cols] = gated[:16]
        halo_s[1, :, cols] = gated[rows - 16:]

    def halo(base, act):
        def left_send():
            return rc(halo_s.at[base], halo_r.at[base + 1], h_ss.at[base], h_rs.at[base + 1],
                      lax.rem(me + S - 1, S), dp)

        def right_send():
            return rc(halo_s.at[base + 1], halo_r.at[base], h_ss.at[base + 1], h_rs.at[base],
                      lax.rem(me + 1, S), dp)

        @pl.when(me > 0)
        def _():
            if act == "start":
                left_send().start()
            elif act == "wait":
                rc(halo_s.at[base + 1], halo_r.at[base], h_ss.at[base + 1], h_rs.at[base],
                   lax.rem(me + S - 1, S), dp).wait_recv()
            else:
                left_send().wait_send()

        @pl.when(me < S - 1)
        def _():
            if act == "start":
                right_send().start()
            elif act == "wait":
                rc(halo_s.at[base], halo_r.at[base + 1], h_ss.at[base], h_rs.at[base + 1],
                   lax.rem(me + 1, S), dp).wait_recv()
            else:
                right_send().wait_send()

    def place(base, buf):
        @pl.when(me > 0)
        def _():
            buf[0:16] = halo_r[base].astype(F32)

        @pl.when(me == 0)
        def _():
            buf[0:16] = jnp.zeros((16, model), F32)

        @pl.when(me < S - 1)
        def _():
            buf[16 + rows:32 + rows] = halo_r[base + 1].astype(F32)

        @pl.when(me == S - 1)
        def _():
            buf[16 + rows:32 + rows] = jnp.zeros((16, model), F32)

    halo(0, "start")
    halo(0, "wait")
    place(0, gp)

    LB = 128

    def forward_block(n, c):
        cols = pl.ds(pl.multiple_of(n * LB, LB), LB)
        acc = jnp.zeros((rows, LB), F32)
        for k in range(KW):
            acc = acc + dkf[k:k + 1, cols] * gp[k + 1:k + 1 + rows, cols]
        sg = sigmoid(acc)
        act_ref[:, cols] = (acc * sg).astype(BF16)
        gc = (gact_ref[:, cols] * sg * (1.0 + acc * (1.0 - sg))).astype(BF16)
        cp[16:16 + rows, cols] = gc.astype(F32)
        halo_s[2, :, cols] = gc[:16]
        halo_s[3, :, cols] = gc[rows - 16:]
        return c

    lax.fori_loop(0, model // LB, forward_block, 0)
    halo(2, "start")

    def kernel_block(n, c):
        cols = pl.ds(pl.multiple_of(n * LB, LB), LB)
        gc = cp[16:16 + rows, cols]
        for k in range(KW):
            gkl[k:k + 1, cols] = jnp.sum(
                gp[k + 1:k + 1 + rows, cols] * gc, axis=0, keepdims=True
            )
        gkl[KW:KW + 1, cols] = jnp.zeros((1, LB), F32)
        return c

    lax.fori_loop(0, model // LB, kernel_block, 0)

    kc = gk1s.shape[2]
    across = model // kc
    for j in range(S):
        r0, c0 = (j // across) * 8, (j % across) * kc
        gk1s[j] = gkl[r0:r0 + 8, c0:c0 + kc]

    def k1(j, src):
        return rc(gk1s.at[j], gk1r.at[src], k1_ss.at[j], k1_rs.at[src], j, dp)

    peers(lambda j: k1(j, me).start(), S, me)
    gk1r[me] = gk1s[me]

    lo_ref[...] = (
        mid_ref[...].astype(F32)
        + jnp.dot(act_ref[...], co_ref[...], preferred_element_type=F32)
    ).astype(BF16)

    halo(2, "wait")
    place(2, cp)

    peers(lambda j: k1(j, j).wait_recv(), S, me)
    gk2s[...] = jnp.sum(gk1r[...], axis=0)

    def k2(j, src):
        return rc(gk2s, gk2r.at[src], k2_ss.at[j], k2_rs.at[src], me, j)

    peers(lambda j: k2(j, dp).start(), DPN, dp)
    gk2r[dp] = gk2s[...]

    def backward_block(n, c):
        cols = pl.ds(pl.multiple_of(n * LB, LB), LB)
        acc = jnp.zeros((rows, LB), F32)
        for k in range(KW):
            acc = acc + dkf[k:k + 1, cols] * cp[31 - k:31 - k + rows, cols]
        gate = gate_ref[:, cols]
        first = acc * gate
        gproj_ref[:, cols] = first.astype(BF16)
        gproj_ref[:, pl.ds(pl.multiple_of(model + n * LB, LB), LB)] = (
            first * val_ref[:, cols] * (1.0 - gate)
        ).astype(BF16)
        return c

    lax.fori_loop(0, model // LB, backward_block, 0)

    peers(lambda j: k2(j, j).wait_recv(), DPN, dp)
    gk3r[me] = jnp.sum(gk2r[...], axis=0)

    def k3(j, src):
        return rc(gk3r.at[src], gk3r.at[src], k3_ss.at[j], k3_rs.at[src], j, dp)

    peers(lambda j: k3(j, me).start(), S, me)

    gn = jnp.zeros((rows, model), F32)
    for n in range(2 * count):
        gn = gn + lax.dot_general(
            gproj_ref[:, n * wide_cols:(n + 1) * wide_cols], weights(n),
            (((1,), (1,)), ((), ())), preferred_element_type=F32,
        )
    wide = mid_ref[...].astype(F32)
    centered = wide - jnp.mean(wide, axis=1, keepdims=True)
    rscale = lax.rsqrt(jnp.mean(centered * centered, axis=1, keepdims=True) + EPS)
    hat = centered * rscale
    dh = gn * ng_ref[...]
    inner = (
        dh
        - jnp.mean(dh, axis=1, keepdims=True)
        - hat * jnp.mean(dh * hat, axis=1, keepdims=True)
    )
    gm = (ct_ref[...].astype(F32) + rscale * inner).astype(BF16)
    gm_ref[...] = gm

    att_t = att_ref[...].T
    nc = model // DPN
    orow = go_ref.shape[0]
    for d in range(DPN):
        piece = jnp.dot(att_t, gm[:, d * nc:(d + 1) * nc], preferred_element_type=F32)
        gods[d] = piece.astype(BF16).reshape(S, orow, nc)

    def gd(j, src):
        return rc(gods.at[j], godr.at[src], gd_ss.at[j], gd_rs.at[src], me, j)

    peers(lambda j: gd(j, dp).start(), DPN, dp)
    godr[dp] = gods[dp]
    peers(lambda j: gd(j, j).wait_recv(), DPN, dp)

    def sum_dp(j, c):
        acc = godr[0, j].astype(F32)
        for d in range(1, DPN):
            acc = acc + godr[d, j].astype(F32)
        gos[j] = acc.astype(BF16)
        return c

    lax.fori_loop(0, S, sum_dp, 0)

    def go(j, src):
        return rc(gos.at[j], gor.at[src], g_ss.at[j], g_rs.at[src], j, dp)

    peers(lambda j: go(j, me).start(), S, me)
    gor[me] = gos[me]

    peers(lambda j: k3(j, j).wait_recv(), S, me)
    for j in range(S):
        r0, c0 = (j // across) * 8, (j % across) * kc
        n = min(8, KW - r0)
        gk_ref[r0:r0 + n, c0:c0 + kc] = gk3r[j][:n]

    peers(lambda j: go(j, j).wait_recv(), S, me)
    acc = gor[0].astype(F32)
    for j in range(1, S):
        acc = acc + gor[j].astype(F32)
    gofr[dp] = acc

    def gf(j, src):
        return rc(gofr.at[src], gofr.at[src], gf_ss.at[j], gf_rs.at[src], me, j)

    peers(lambda j: gf(j, dp).start(), DPN, dp)

    def close(j):
        kv_copy(j, me).wait_send()
        q_copy(j, me).wait_send()
        at_copy(j, me).wait_send()
        k1(j, me).wait_send()
        k3(j, me).wait_send()
        go(j, me).wait_send()

    peers(close, S, me)
    for o, order in enumerate((order_a, order_b)):
        for n in range(len(bits)):
            for r in subsets(order, n):
                w_copy(o, r, order[n]).wait_send()
    if share == 2:
        for r in range(1, S):
            sib_copy(r).wait_send()
    halo(0, "close")
    halo(2, "close")

    peers(lambda j: gf(j, j).wait_recv(), DPN, dp)
    for d in range(DPN):
        go_ref[:, d * nc:(d + 1) * nc] = gofr[d]

    def close_dp(j):
        k2(j, dp).wait_send()
        gd(j, dp).wait_send()
        gf(j, dp).wait_send()

    peers(close_dp, DPN, dp)


def body(queries, keys, values, residual, out_proj, conv_in, conv_out, depth_kernel, norm_gain,
         cotangent):
    S = lax.axis_size("seq")
    DPN = lax.axis_size("dp")
    batch, rows, width = queries.shape
    model = residual.shape[2]
    group = S // HEADS
    part = rows // group
    cw = conv_in.shape[1]
    kc = 32 * model // (8 * S)
    orow = width // S
    nc = model // DPN
    V = pltpu.VMEM
    D = pltpu.SemaphoreType.DMA
    wide = V((rows, model), F32)
    slim = V((rows, model), BF16)
    scratch = [
        V((HEADS, rows, 2 * DH), BF16), V((S, rows, 2 * DH), BF16),
        V((S, part, 2 * DH), BF16), V((S, part, 2 * DH), BF16),
        V((S, part, 2 * DH), BF16), V((S, part, 2 * DH), BF16),
        V((S, model, cw), BF16),
        V((rows, width), BF16), slim, wide, wide, wide, slim, slim,
        V((rows + 32, model), F32), V((rows + 32, model), F32), V((rows, 2 * model), BF16),
        V((4, 16, model), BF16), V((4, 16, model), BF16), V((32, model), F32),
        V((32, model), F32), V((S, 8, kc), F32), V((S, 8, kc), F32),
        V((8, kc), F32), V((DPN, 8, kc), F32), V((S, 8, kc), F32),
        V((DPN, S, orow, nc), BF16), V((DPN, S, orow, nc), BF16),
        V((S, orow, nc), BF16), V((S, orow, nc), BF16), V((DPN, orow, nc), F32),
        D((S,)), D((S,)), D((S,)), D((S,)), D((S,)), D((S,)), D((2, S)), D((2, S)), D((S,)), D((S,)),
        D((4,)), D((4,)), D((S,)), D((S,)), D((DPN,)), D((DPN,)), D((S,)), D((S,)),
        D((DPN,)), D((DPN,)), D((S,)), D((S,)), D((DPN,)), D((DPN,)),
    ]
    vm = pl.BlockSpec(memory_space=pltpu.VMEM)
    lo, gm, go, gk = pl.pallas_call(
        functools.partial(kernel, S, DPN),
        out_shape=[
            jax.ShapeDtypeStruct((rows, model), BF16),
            jax.ShapeDtypeStruct((rows, model), BF16),
            jax.ShapeDtypeStruct((orow, model), F32),
            jax.ShapeDtypeStruct((KW, model), F32),
        ],
        in_specs=[vm] * 10,
        out_specs=[vm] * 4,
        scratch_shapes=scratch,
        compiler_params=pltpu.CompilerParams(
            collective_id=0, has_side_effects=True, vmem_limit_bytes=60 * 1024 * 1024
        ),
    )(
        queries[0], keys[0], values[0], residual[0], out_proj, conv_in, conv_out, depth_kernel,
        norm_gain.reshape(1, model), cotangent[0],
    )
    return lo[None], gm[None], go, gk


def solution(mesh):
    return jax.shard_map(
        body,
        mesh=mesh,
        in_specs=(
            P("dp", "seq", None),
            P("dp", "seq", None),
            P("dp", "seq", None),
            P("dp", "seq", None),
            P(),
            P(None, "seq"),
            P(),
            P(),
            P(),
            P("dp", "seq", None),
        ),
        out_specs=(P("dp", "seq", None), P("dp", "seq", None), P("seq", None), P()),
        check_vma=False,
    )
```

```python
import functools

import jax
import jax.numpy as jnp
from jax import lax
from jax.experimental import pallas as pl
from jax.experimental.pallas import tpu as pltpu
from jax.sharding import PartitionSpec as P

HEADS = 8
DH = 64
KW = 31
EPS = 1e-05
F32 = jnp.float32
BF16 = jnp.bfloat16
MESH = pl.DeviceIdType.MESH


def sigmoid(x):
    return 1.0 / (1.0 + jnp.exp(-x))


def toggled(me, r):
    out = me
    b = 1
    while b <= r:
        if r & b:
            out = out + b * (1 - 2 * ((me // b) % 2))
        b *= 2
    return out


def kernel(
    S, DPN,
    q_in, k_in, v_in, res_in, op_in, ci_in, co_in, dk_in, ng_in, ct_in,
    lo_out, gm_out, go_out, gk_out,
    q_ref, k_ref, v_ref, res_ref, op_ref, co_ref, dk_ref, ng_ref, ct_ref,
    lo_ref, gm_ref, go_ref, gk_ref, in_sem, out_sem, fw_ss,
    kvs, kvr, qs, qr, ats, atr, wf,
    att_ref, mid_ref, val_ref, gate_ref, gact_ref, act_ref, gcb_ref, gp, cp, gproj_ref,
    halo_s, halo_r, dkf,
    gkl, gk1s, gk1r, gk2s, gk2r, gk3r,
    gods, godr, gos, gor, gofr,
    kv_ss, kv_rs, q_ss, q_rs, at_ss, at_rs, w_ss, w_rs, sb_ss, sb_rs,
    h_ss, h_rs, k1_ss, k1_rs, k2_ss, k2_rs, k3_ss, k3_rs,
    gd_ss, gd_rs, g_ss, g_rs, gf_ss, gf_rs,
):
    me = lax.axis_index("seq")
    dp = lax.axis_index("dp")
    rows, model = res_in.shape
    group = S // HEADS
    part = rows // group
    cw = ci_in.shape[1]
    member = lax.rem(me, group)
    lead = me - member

    loads = [
        pltpu.make_async_copy(src, dst, in_sem.at[n])
        for n, (src, dst) in enumerate([
            (q_in, q_ref), (k_in, k_ref), (v_in, v_ref), (ci_in, wf.at[me]), (ct_in, ct_ref),
            (co_in, co_ref), (op_in, op_ref), (res_in, res_ref), (ng_in, ng_ref),
            (dk_in, dk_ref),
        ])
    ]
    for load in loads:
        load.start()
    stores = [
        pltpu.make_async_copy(src, dst, out_sem.at[n])
        for n, (src, dst) in enumerate([
            (lo_ref, lo_out), (gm_ref, gm_out), (go_ref, go_out), (gk_ref, gk_out),
        ])
    ]
    bits = []
    b = S // 2
    while b >= 1:
        bits.append(b)
        b //= 2
    swapped = bits[:-2] + [bits[-1], bits[-2]]
    back = [bits[-1], bits[-2]] + bits[:-2]
    turned = [bits[-2], bits[-1]] + bits[:-2]
    orders = [bits, bits, bits, swapped, swapped, swapped, back, turned]
    pieces = len(orders)

    def rc(src, dst, ss, rs, seq_id, dp_id):
        return pltpu.make_async_remote_copy(
            src_ref=src, dst_ref=dst, send_sem=ss, recv_sem=rs,
            device_id=(dp_id, seq_id), device_id_type=MESH,
        )

    def peers(fn, n, mine):
        def step(i, c):
            fn(lax.rem(mine + i, n))
            return c
        lax.fori_loop(1, n, step, 0)

    barrier = pltpu.get_barrier_semaphore()

    def hello_seq(j):
        pl.semaphore_signal(barrier, inc=1, device_id=(dp, j), device_id_type=MESH)

    def hello_dp(j):
        pl.semaphore_signal(barrier, inc=1, device_id=(j, me), device_id_type=MESH)

    peers(hello_seq, S, me)
    peers(hello_dp, DPN, dp)

    for load in loads[:3]:
        load.wait()

    zeros64 = jnp.zeros((part, DH), BF16)
    for h in range(HEADS):
        cols = slice(h * DH, (h + 1) * DH)
        kvs[h] = jnp.concatenate([k_ref[:, cols], v_ref[:, cols]], axis=1)
        for g in range(group):
            piece = q_ref[g * part:(g + 1) * part, cols] * jnp.asarray(DH ** -0.5, BF16)
            qs[h * group + g] = jnp.concatenate([piece, zeros64], axis=1)
    pl.semaphore_wait(barrier, S - 1 + DPN - 1)

    def kv_copy(h):
        return rc(kvs.at[h], kvr.at[me], kv_ss.at[h], kv_rs.at[me], h * group + member, dp)

    def kv_hand(src, i, e):
        where = kvr.at[src]
        return rc(where, where, fw_ss.at[i, e], kv_rs.at[src],
                  lead + lax.rem(member + e, group), dp)

    def kv_wait(src, peer):
        where = kvr.at[src]
        rc(where, where, kv_ss.at[0], kv_rs.at[src], peer, dp).wait_recv()

    def q_copy(j, src):
        return rc(qs.at[j], qr.at[src], q_ss.at[j], q_rs.at[src], j, dp)

    mine = me // group
    peers(lambda h: kv_copy(h).start(), HEADS, mine)
    peers(lambda j: q_copy(j, me).start(), S, me)
    kvr[me] = kvs[mine]
    qr[me] = qs[me]
    for e in range(1, group):
        kv_hand(me, 0, e).start()
    loads[3].wait()

    share = 2 if DPN % 2 == 0 else 1
    core = lax.rem(dp, share)
    sib = dp + 1 - 2 * core
    half = model // share
    sub = half // pieces

    def w_copy(o, r, b):
        chunk = toggled(me, r)
        begin = pl.multiple_of(core * half + o * sub, sub)
        where = wf.at[chunk, pl.ds(begin, sub)]
        return rc(where, where, w_ss.at[o, r + b], w_rs.at[o, r + b], toggled(me, b), dp)

    def sib_copy(r):
        where = wf.at[toggled(me, r), pl.ds(pl.multiple_of(core * half, half), half)]
        return rc(where, where, sb_ss.at[r], sb_rs.at[r], me, sib)

    def sib_recv(r):
        where = wf.at[toggled(me, r), pl.ds(pl.multiple_of((1 - core) * half, half), half)]
        return rc(where, where, sb_ss.at[r], sb_rs.at[r], me, sib)

    def subsets(order, n):
        out = [0]
        for b in order[:n]:
            out = out + [r + b for r in out]
        return out

    def w_recv_wait(o, r, b):
        chunk = toggled(me, r + b)
        begin = pl.multiple_of(core * half + o * sub, sub)
        where = wf.at[chunk, pl.ds(begin, sub)]
        rc(where, where, w_ss.at[o, r + b], w_rs.at[o, r + b], toggled(me, b), dp).wait_recv()

    done = set()

    def gather_step(n):
        for o, order in enumerate(orders):
            if n > 0:
                for r in subsets(order, n - 1):
                    w_recv_wait(o, r, order[n - 1])
            if n < len(bits):
                for r in subsets(order, n):
                    w_copy(o, r, order[n]).start()
        if share == 2:
            both = set.intersection(*[set(subsets(order, n)) for order in orders])
            for r in sorted(both - done - {0}):
                sib_copy(r).start()
                done.add(r)

    gather_step(0)

    def hand(i, c):
        src = lax.rem(mine + i, HEADS) * group + member
        kv_wait(src, src)
        for e in range(1, group):
            kv_hand(src, i, e).start()
        return c

    lax.fori_loop(1, HEADS, hand, 0)
    peers(lambda j: q_copy(j, j).wait_recv(), S, me)

    def handed(i, c):
        for e in range(1, group):
            giver = lax.rem(member + e, group)
            kv_wait(i * group + giver, lead + giver)
        return c

    lax.fori_loop(0, HEADS, handed, 0)
    gather_step(1)

    owners = max(1, 256 // part)
    blocks = S // owners
    kv = kvr[...].reshape(S * rows, 2 * DH)

    def at_copy(j, src):
        return rc(ats.at[j], atr.at[src], at_ss.at[j], at_rs.at[src], j, dp)

    def attend(i, c):
        first = i * owners
        q = qr[pl.ds(first, owners)].reshape(owners * part, 2 * DH)
        s = lax.dot_general(q, kv, (((1,), (1,)), ((), ())), preferred_element_type=F32)
        top = jnp.max(s, axis=1, keepdims=True)
        e = jnp.exp(s - top)
        total = jnp.sum(e, axis=1, keepdims=True)
        mixed = jnp.dot(e.astype(BF16), kv, preferred_element_type=F32)
        out = (mixed / total).astype(BF16).reshape(owners, part, 2 * DH)
        ats[pl.ds(first, owners)] = out

        def send(n, c2):
            j = first + n

            @pl.when(j != me)
            def _():
                at_copy(j, me).start()
            return c2
        lax.fori_loop(0, owners, send, 0)
        return c

    lax.fori_loop(0, blocks // 2, attend, 0)
    gather_step(2)
    lax.fori_loop(blocks // 2, blocks, attend, 0)
    for n in range(3, len(bits)):
        gather_step(n)
    for load in loads[4:]:
        load.wait()
    atr[me] = ats[me]
    dkf[0:KW] = dk_ref[...].astype(F32)

    ct = ct_ref[...]
    gact_ref[...] = lax.dot_general(
        ct, co_ref[...], (((1,), (1,)), ((), ())), preferred_element_type=F32
    )

    def wait_at(j):
        at_copy(j, j).wait_recv()

    peers(wait_at, S, me)
    for g in range(group):
        for h in range(0, HEADS, 2):
            left = atr[h * group + g][:, DH:]
            right = atr[(h + 1) * group + g][:, DH:]
            att_ref[g * part:(g + 1) * part, h * DH:(h + 2) * DH] = jnp.concatenate(
                [left, right], axis=1
            )
    mid = (
        res_ref[...].astype(F32)
        + jnp.dot(att_ref[...], op_ref[...], preferred_element_type=F32)
    ).astype(BF16)
    mid_ref[...] = mid
    wide = mid.astype(F32)
    centered = wide - jnp.mean(wide, axis=1, keepdims=True)
    rscale = lax.rsqrt(jnp.mean(centered * centered, axis=1, keepdims=True) + EPS)
    gain = ng_ref[...]
    normed = (centered * rscale * gain).astype(BF16)

    gather_step(len(bits))
    if share == 2:
        for r in range(1, S):
            sib_recv(r).wait_recv()

    per = max(1, 256 // cw)
    wide_cols = per * cw

    def weights(n):
        return jnp.concatenate([wf[n * per + i] for i in range(per)], axis=1)

    count = model // wide_cols
    for n in range(count):
        cols = slice(n * wide_cols, (n + 1) * wide_cols)
        value = jnp.dot(normed, weights(n), preferred_element_type=F32)
        gate = sigmoid(jnp.dot(normed, weights(count + n), preferred_element_type=F32))
        val_ref[:, cols] = value
        gate_ref[:, cols] = gate
        gated = (value * gate).astype(BF16)
        gp[16:16 + rows, cols] = gated.astype(F32)
        halo_s[0, :, cols] = gated[:16]
        halo_s[1, :, cols] = gated[rows - 16:]

    def halo(base, act):
        def left_send():
            return rc(halo_s.at[base], halo_r.at[base + 1], h_ss.at[base], h_rs.at[base + 1],
                      lax.rem(me + S - 1, S), dp)

        def right_send():
            return rc(halo_s.at[base + 1], halo_r.at[base], h_ss.at[base + 1], h_rs.at[base],
                      lax.rem(me + 1, S), dp)

        @pl.when(me > 0)
        def _():
            if act == "start":
                left_send().start()
            elif act == "wait":
                rc(halo_s.at[base + 1], halo_r.at[base], h_ss.at[base + 1], h_rs.at[base],
                   lax.rem(me + S - 1, S), dp).wait_recv()
            else:
                left_send().wait_send()

        @pl.when(me < S - 1)
        def _():
            if act == "start":
                right_send().start()
            elif act == "wait":
                rc(halo_s.at[base], halo_r.at[base + 1], h_ss.at[base], h_rs.at[base + 1],
                   lax.rem(me + 1, S), dp).wait_recv()
            else:
                right_send().wait_send()

    def place(base, buf):
        @pl.when(me > 0)
        def _():
            buf[0:16] = halo_r[base].astype(F32)

        @pl.when(me == 0)
        def _():
            buf[0:16] = jnp.zeros((16, model), F32)

        @pl.when(me < S - 1)
        def _():
            buf[16 + rows:32 + rows] = halo_r[base + 1].astype(F32)

        @pl.when(me == S - 1)
        def _():
            buf[16 + rows:32 + rows] = jnp.zeros((16, model), F32)

    halo(0, "start")
    halo(0, "wait")
    place(0, gp)

    LB = 128

    def forward_block(n, c):
        cols = pl.ds(pl.multiple_of(n * LB, LB), LB)
        acc = jnp.zeros((rows, LB), F32)
        for k in range(KW):
            acc = acc + dkf[k:k + 1, cols] * gp[k + 1:k + 1 + rows, cols]
        sg = sigmoid(acc)
        act_ref[:, cols] = (acc * sg).astype(BF16)
        gc = (gact_ref[:, cols] * sg * (1.0 + acc * (1.0 - sg))).astype(BF16)
        cp[16:16 + rows, cols] = gc.astype(F32)
        halo_s[2, :, cols] = gc[:16]
        halo_s[3, :, cols] = gc[rows - 16:]
        return c

    lax.fori_loop(0, model // LB, forward_block, 0)
    halo(2, "start")

    def kernel_block(n, c):
        cols = pl.ds(pl.multiple_of(n * LB, LB), LB)
        gc = cp[16:16 + rows, cols]
        for k in range(KW):
            gkl[k:k + 1, cols] = jnp.sum(
                gp[k + 1:k + 1 + rows, cols] * gc, axis=0, keepdims=True
            )
        gkl[KW:KW + 1, cols] = jnp.zeros((1, LB), F32)
        return c

    lax.fori_loop(0, model // LB, kernel_block, 0)

    kc = gk1s.shape[2]
    across = model // kc
    for j in range(S):
        r0, c0 = (j // across) * 8, (j % across) * kc
        gk1s[j] = gkl[r0:r0 + 8, c0:c0 + kc]

    def k1(j, src):
        return rc(gk1s.at[j], gk1r.at[src], k1_ss.at[j], k1_rs.at[src], j, dp)

    peers(lambda j: k1(j, me).start(), S, me)
    gk1r[me] = gk1s[me]

    lo_ref[...] = (
        mid_ref[...].astype(F32)
        + jnp.dot(act_ref[...], co_ref[...], preferred_element_type=F32)
    ).astype(BF16)
    stores[0].start()

    halo(2, "wait")
    place(2, cp)

    peers(lambda j: k1(j, j).wait_recv(), S, me)
    gk2s[...] = jnp.sum(gk1r[...], axis=0)

    def k2(j, src):
        return rc(gk2s, gk2r.at[src], k2_ss.at[j], k2_rs.at[src], me, j)

    peers(lambda j: k2(j, dp).start(), DPN, dp)
    gk2r[dp] = gk2s[...]

    def backward_block(n, c):
        cols = pl.ds(pl.multiple_of(n * LB, LB), LB)
        acc = jnp.zeros((rows, LB), F32)
        for k in range(KW):
            acc = acc + dkf[k:k + 1, cols] * cp[31 - k:31 - k + rows, cols]
        gate = gate_ref[:, cols]
        first = acc * gate
        gproj_ref[:, cols] = first.astype(BF16)
        gproj_ref[:, pl.ds(pl.multiple_of(model + n * LB, LB), LB)] = (
            first * val_ref[:, cols] * (1.0 - gate)
        ).astype(BF16)
        return c

    lax.fori_loop(0, model // LB, backward_block, 0)

    peers(lambda j: k2(j, j).wait_recv(), DPN, dp)
    gk3r[me] = jnp.sum(gk2r[...], axis=0)

    def k3(j, src):
        return rc(gk3r.at[src], gk3r.at[src], k3_ss.at[j], k3_rs.at[src], j, dp)

    peers(lambda j: k3(j, me).start(), S, me)

    gn = jnp.zeros((rows, model), F32)
    for n in range(2 * count):
        gn = gn + lax.dot_general(
            gproj_ref[:, n * wide_cols:(n + 1) * wide_cols], weights(n),
            (((1,), (1,)), ((), ())), preferred_element_type=F32,
        )
    wide = mid_ref[...].astype(F32)
    centered = wide - jnp.mean(wide, axis=1, keepdims=True)
    rscale = lax.rsqrt(jnp.mean(centered * centered, axis=1, keepdims=True) + EPS)
    hat = centered * rscale
    dh = gn * ng_ref[...]
    inner = (
        dh
        - jnp.mean(dh, axis=1, keepdims=True)
        - hat * jnp.mean(dh * hat, axis=1, keepdims=True)
    )
    gm = (ct_ref[...].astype(F32) + rscale * inner).astype(BF16)
    gm_ref[...] = gm
    stores[1].start()

    att_t = att_ref[...].T
    nc = model // DPN
    orow = go_ref.shape[0]
    for d in range(DPN):
        piece = jnp.dot(att_t, gm[:, d * nc:(d + 1) * nc], preferred_element_type=F32)
        gods[d] = piece.astype(BF16).reshape(S, orow, nc)

    def gd(j, src):
        return rc(gods.at[j], godr.at[src], gd_ss.at[j], gd_rs.at[src], me, j)

    peers(lambda j: gd(j, dp).start(), DPN, dp)
    godr[dp] = gods[dp]
    peers(lambda j: gd(j, j).wait_recv(), DPN, dp)

    def sum_dp(j, c):
        acc = godr[0, j].astype(F32)
        for d in range(1, DPN):
            acc = acc + godr[d, j].astype(F32)
        gos[j] = acc.astype(BF16)
        return c

    lax.fori_loop(0, S, sum_dp, 0)

    def go(j, src):
        return rc(gos.at[j], gor.at[src], g_ss.at[j], g_rs.at[src], j, dp)

    peers(lambda j: go(j, me).start(), S, me)
    gor[me] = gos[me]

    peers(lambda j: k3(j, j).wait_recv(), S, me)
    for j in range(S):
        r0, c0 = (j // across) * 8, (j % across) * kc
        n = min(8, KW - r0)
        gk_ref[r0:r0 + n, c0:c0 + kc] = gk3r[j][:n]

    stores[3].start()

    peers(lambda j: go(j, j).wait_recv(), S, me)
    acc = gor[0].astype(F32)
    for j in range(1, S):
        acc = acc + gor[j].astype(F32)
    gofr[dp] = acc

    def gf(j, src):
        return rc(gofr.at[src], gofr.at[src], gf_ss.at[j], gf_rs.at[src], me, j)

    peers(lambda j: gf(j, dp).start(), DPN, dp)

    def close(j):
        q_copy(j, me).wait_send()
        at_copy(j, me).wait_send()
        k1(j, me).wait_send()
        k3(j, me).wait_send()
        go(j, me).wait_send()

    peers(close, S, me)
    peers(lambda h: kv_copy(h).wait_send(), HEADS, mine)

    def close_hand(i, c):
        src = lax.rem(mine + i, HEADS) * group + member
        for e in range(1, group):
            kv_hand(src, i, e).wait_send()
        return c

    lax.fori_loop(0, HEADS, close_hand, 0)
    for o, order in enumerate(orders):
        for n in range(len(bits)):
            for r in subsets(order, n):
                w_copy(o, r, order[n]).wait_send()
    if share == 2:
        for r in range(1, S):
            sib_copy(r).wait_send()
    halo(0, "close")
    halo(2, "close")

    peers(lambda j: gf(j, j).wait_recv(), DPN, dp)
    for d in range(DPN):
        go_ref[:, d * nc:(d + 1) * nc] = gofr[d]
    stores[2].start()

    def close_dp(j):
        k2(j, dp).wait_send()
        gd(j, dp).wait_send()
        gf(j, dp).wait_send()

    peers(close_dp, DPN, dp)
    for store in stores:
        store.wait()


def hand_on(a, b, c, d, a_out, b_out, c_out, d_out, ab, bb, cb, db, in_sem, out_sem):
    held = [ab, bb, cb, db]
    loads = [
        pltpu.make_async_copy(src, buf, in_sem.at[n])
        for n, (src, buf) in enumerate(zip([a, b, c, d], held))
    ]
    stores = [
        pltpu.make_async_copy(buf, dst, out_sem.at[n])
        for n, (buf, dst) in enumerate(zip(held, [a_out, b_out, c_out, d_out]))
    ]
    for load in loads:
        load.start()
    for load, store in zip(loads, stores):
        load.wait()
        store.start()
    for store in stores:
        store.wait()


def body(queries, keys, values, residual, out_proj, conv_in, conv_out, depth_kernel, norm_gain,
         cotangent):
    S = lax.axis_size("seq")
    DPN = lax.axis_size("dp")
    batch, rows, width = queries.shape
    model = residual.shape[2]
    group = S // HEADS
    part = rows // group
    cw = conv_in.shape[1]
    kc = 32 * model // (8 * S)
    orow = width // S
    nc = model // DPN
    V = pltpu.VMEM
    D = pltpu.SemaphoreType.DMA
    wide = V((rows, model), F32)
    slim = V((rows, model), BF16)
    scratch = [
        V((rows, width), BF16), V((rows, width), BF16), V((rows, width), BF16), slim,
        V((width, model), BF16), V((model, model), BF16), V((KW, model), BF16),
        V((1, model), F32), slim,
        slim, slim, V((orow, model), F32), V((KW, model), F32),
        D((10,)), D((4,)), D((HEADS, group)),
        V((HEADS, rows, 2 * DH), BF16), V((S, rows, 2 * DH), BF16),
        V((S, part, 2 * DH), BF16), V((S, part, 2 * DH), BF16),
        V((S, part, 2 * DH), BF16), V((S, part, 2 * DH), BF16),
        V((S, model, cw), BF16),
        V((rows, width), BF16), slim, wide, wide, wide, slim, slim,
        V((rows + 32, model), F32), V((rows + 32, model), F32), V((rows, 2 * model), BF16),
        V((4, 16, model), BF16), V((4, 16, model), BF16), V((32, model), F32),
        V((32, model), F32), V((S, 8, kc), F32), V((S, 8, kc), F32),
        V((8, kc), F32), V((DPN, 8, kc), F32), V((S, 8, kc), F32),
        V((DPN, S, orow, nc), BF16), V((DPN, S, orow, nc), BF16),
        V((S, orow, nc), BF16), V((S, orow, nc), BF16), V((DPN, orow, nc), F32),
        D((HEADS,)), D((S,)), D((S,)), D((S,)), D((S,)), D((S,)), D((8, S)), D((8, S)), D((S,)), D((S,)),
        D((4,)), D((4,)), D((S,)), D((S,)), D((DPN,)), D((DPN,)), D((S,)), D((S,)),
        D((DPN,)), D((DPN,)), D((S,)), D((S,)), D((DPN,)), D((DPN,)),
    ]
    anywhere = pl.BlockSpec(memory_space=pl.ANY)
    shapes = [
        jax.ShapeDtypeStruct((rows, model), BF16),
        jax.ShapeDtypeStruct((rows, model), BF16),
        jax.ShapeDtypeStruct((orow, model), F32),
        jax.ShapeDtypeStruct((KW, model), F32),
    ]
    results = pl.pallas_call(
        functools.partial(kernel, S, DPN),
        out_shape=shapes,
        in_specs=[anywhere] * 10,
        out_specs=[anywhere] * 4,
        scratch_shapes=scratch,
        compiler_params=pltpu.CompilerParams(
            collective_id=0, has_side_effects=True, vmem_limit_bytes=60 * 1024 * 1024
        ),
    )(
        queries[0], keys[0], values[0], residual[0], out_proj, conv_in, conv_out, depth_kernel,
        norm_gain.reshape(1, model), cotangent[0],
    )
    lo, gm, go, gk = pl.pallas_call(
        hand_on,
        out_shape=shapes,
        in_specs=[anywhere] * 4,
        out_specs=[anywhere] * 4,
        scratch_shapes=[V(x.shape, x.dtype) for x in shapes] + [D((4,)), D((4,))],
    )(*results)
    return lo[None], gm[None], go, gk


def solution(mesh):
    return jax.shard_map(
        body,
        mesh=mesh,
        in_specs=(
            P("dp", "seq", None),
            P("dp", "seq", None),
            P("dp", "seq", None),
            P("dp", "seq", None),
            P(),
            P(None, "seq"),
            P(),
            P(),
            P(),
            P("dp", "seq", None),
        ),
        out_specs=(P("dp", "seq", None), P("dp", "seq", None), P("seq", None), P()),
        check_vma=False,
    )
```

```python
import functools

import jax
import jax.numpy as jnp
from jax import lax
from jax.experimental import pallas as pl
from jax.experimental.pallas import tpu as pltpu
from jax.sharding import PartitionSpec as P

HEADS = 8
DH = 64
KW = 31
EPS = 1e-05
F32 = jnp.float32
BF16 = jnp.bfloat16
MESH = pl.DeviceIdType.MESH


def sigmoid(x):
    return 1.0 / (1.0 + jnp.exp(-x))


def toggled(me, r):
    out = me
    b = 1
    while b <= r:
        if r & b:
            out = out + b * (1 - 2 * ((me // b) % 2))
        b *= 2
    return out


def kernel(
    S, DPN,
    q_in, k_in, v_in, res_in, op_in, ci_in, co_in, dk_in, ng_in, ct_in,
    lo_out, gm_out, go_out, gk_out,
    q_ref, k_ref, v_ref, res_ref, op_ref, co_ref, dk_ref, ng_ref, ct_ref,
    lo_ref, gm_ref, go_ref, gk_ref, in_sem, out_sem, fw_ss,
    kvs, kvr, qs, qr, ats, atr, wf,
    att_ref, mid_ref, val_ref, gate_ref, gact_ref, act_ref, gcb_ref, gp, cp, gproj_ref,
    halo_s, halo_r, dkf,
    gkl, gk1s, gk1r, gk2s, gk2r, gk3r,
    gods, godr, gos, gor, gofr,
    kv_ss, kv_rs, q_ss, q_rs, at_ss, at_rs, w_ss, w_rs, sb_ss, sb_rs,
    h_ss, h_rs, k1_ss, k1_rs, k2_ss, k2_rs, k3_ss, k3_rs,
    gd_ss, gd_rs, g_ss, g_rs, gf_ss, gf_rs,
):
    me = lax.axis_index("seq")
    dp = lax.axis_index("dp")
    rows, model = res_in.shape
    group = S // HEADS
    part = rows // group
    packed = part % 32 == 0
    cw = ci_in.shape[1]
    member = lax.rem(me, group)
    lead = me - member

    loads = [
        pltpu.make_async_copy(src, dst, in_sem.at[n])
        for n, (src, dst) in enumerate([
            (q_in, q_ref), (k_in, k_ref), (v_in, v_ref), (ci_in, wf.at[me]), (ct_in, ct_ref),
            (co_in, co_ref), (op_in, op_ref), (res_in, res_ref), (ng_in, ng_ref),
            (dk_in, dk_ref),
        ])
    ]
    for load in loads:
        load.start()
    stores = [
        pltpu.make_async_copy(src, dst, out_sem.at[n])
        for n, (src, dst) in enumerate([
            (lo_ref, lo_out), (gm_ref, gm_out), (go_ref, go_out), (gk_ref, gk_out),
        ])
    ]
    bits = []
    b = S // 2
    while b >= 1:
        bits.append(b)
        b //= 2
    swapped = bits[:-2] + [bits[-1], bits[-2]]
    back = [bits[-1], bits[-2]] + bits[:-2]
    turned = [bits[-2], bits[-1]] + bits[:-2]
    orders = [bits, bits, bits, swapped, swapped, swapped, back, turned]
    pieces = len(orders)

    def rc(src, dst, ss, rs, seq_id, dp_id):
        return pltpu.make_async_remote_copy(
            src_ref=src, dst_ref=dst, send_sem=ss, recv_sem=rs,
            device_id=(dp_id, seq_id), device_id_type=MESH,
        )

    def peers(fn, n, mine):
        def step(i, c):
            fn(lax.rem(mine + i, n))
            return c
        lax.fori_loop(1, n, step, 0)

    barrier = pltpu.get_barrier_semaphore()

    def hello_seq(j):
        pl.semaphore_signal(barrier, inc=1, device_id=(dp, j), device_id_type=MESH)

    def hello_dp(j):
        pl.semaphore_signal(barrier, inc=1, device_id=(j, me), device_id_type=MESH)

    peers(hello_seq, S, me)
    peers(hello_dp, DPN, dp)

    for load in loads[:3]:
        load.wait()

    zeros64 = jnp.zeros((part, DH), BF16)
    for h in range(HEADS):
        cols = slice(h * DH, (h + 1) * DH)
        kvs[h] = jnp.concatenate([k_ref[:, cols], v_ref[:, cols]], axis=1)
        for g in range(group):
            piece = q_ref[g * part:(g + 1) * part, cols] * jnp.asarray(DH ** -0.5, BF16)
            if packed:
                qs[h * group + g] = jnp.concatenate([piece[:part // 2], piece[part // 2:]], axis=1)
            else:
                qs[h * group + g] = jnp.concatenate([piece, zeros64], axis=1)
    pl.semaphore_wait(barrier, S - 1 + DPN - 1)

    def kv_copy(h):
        return rc(kvs.at[h], kvr.at[me], kv_ss.at[h], kv_rs.at[me], h * group + member, dp)

    def kv_hand(src, i, e):
        where = kvr.at[src]
        return rc(where, where, fw_ss.at[i, e], kv_rs.at[src],
                  lead + lax.rem(member + e, group), dp)

    def kv_wait(src, peer):
        where = kvr.at[src]
        rc(where, where, kv_ss.at[0], kv_rs.at[src], peer, dp).wait_recv()

    def q_copy(j, src):
        return rc(qs.at[j], qr.at[src], q_ss.at[j], q_rs.at[src], j, dp)

    mine = me // group
    peers(lambda h: kv_copy(h).start(), HEADS, mine)
    peers(lambda j: q_copy(j, me).start(), S, me)
    kvr[me] = kvs[mine]
    qr[me] = qs[me]
    for e in range(1, group):
        kv_hand(me, 0, e).start()
    loads[3].wait()

    share = 2 if DPN % 2 == 0 else 1
    core = lax.rem(dp, share)
    sib = dp + 1 - 2 * core
    half = model // share
    sub = half // pieces

    def w_copy(o, r, b):
        chunk = toggled(me, r)
        begin = pl.multiple_of(core * half + o * sub, sub)
        where = wf.at[chunk, pl.ds(begin, sub)]
        return rc(where, where, w_ss.at[o, r + b], w_rs.at[o, r + b], toggled(me, b), dp)

    def sib_copy(r):
        where = wf.at[toggled(me, r), pl.ds(pl.multiple_of(core * half, half), half)]
        return rc(where, where, sb_ss.at[r], sb_rs.at[r], me, sib)

    def sib_recv(r):
        where = wf.at[toggled(me, r), pl.ds(pl.multiple_of((1 - core) * half, half), half)]
        return rc(where, where, sb_ss.at[r], sb_rs.at[r], me, sib)

    def subsets(order, n):
        out = [0]
        for b in order[:n]:
            out = out + [r + b for r in out]
        return out

    def w_recv_wait(o, r, b):
        chunk = toggled(me, r + b)
        begin = pl.multiple_of(core * half + o * sub, sub)
        where = wf.at[chunk, pl.ds(begin, sub)]
        rc(where, where, w_ss.at[o, r + b], w_rs.at[o, r + b], toggled(me, b), dp).wait_recv()

    done = set()

    def gather_step(n):
        for o, order in enumerate(orders):
            if n > 0:
                for r in subsets(order, n - 1):
                    w_recv_wait(o, r, order[n - 1])
            if n < len(bits):
                for r in subsets(order, n):
                    w_copy(o, r, order[n]).start()
        if share == 2:
            both = set.intersection(*[set(subsets(order, n)) for order in orders])
            for r in sorted(both - done - {0}):
                sib_copy(r).start()
                done.add(r)

    gather_step(0)

    def hand(i, c):
        src = lax.rem(mine + i, HEADS) * group + member
        kv_wait(src, src)
        for e in range(1, group):
            kv_hand(src, i, e).start()
        return c

    lax.fori_loop(1, HEADS, hand, 0)
    peers(lambda j: q_copy(j, j).wait_recv(), S, me)

    gather_step(1)

    def handed(i, c):
        for e in range(1, group):
            giver = lax.rem(member + e, group)
            kv_wait(i * group + giver, lead + giver)
        return c

    lax.fori_loop(0, HEADS, handed, 0)
    owners = max(1, 256 // part)
    blocks = S // owners
    kv = kvr[...].reshape(S * rows, 2 * DH)

    def at_copy(j, src):
        return rc(ats.at[j], atr.at[src], at_ss.at[j], at_rs.at[src], j, dp)

    def attend(i, c):
        first = i * owners
        q = qr[pl.ds(first, owners)]
        if packed:
            blank = jnp.zeros((owners, part // 2, DH), BF16)
            q = jnp.concatenate(
                [
                    jnp.concatenate([q[:, :, :DH], blank], axis=2),
                    jnp.concatenate([q[:, :, DH:], blank], axis=2),
                ],
                axis=1,
            )
        q = q.reshape(owners * part, 2 * DH)
        s = lax.dot_general(q, kv, (((1,), (1,)), ((), ())), preferred_element_type=F32)
        top = jnp.max(s, axis=1, keepdims=True)
        e = jnp.exp(s - top)
        total = jnp.sum(e, axis=1, keepdims=True)
        mixed = jnp.dot(e.astype(BF16), kv, preferred_element_type=F32)
        out = (mixed / total).astype(BF16).reshape(owners, part, 2 * DH)
        if packed:
            out = jnp.concatenate([out[:, :part // 2, DH:], out[:, part // 2:, DH:]], axis=2)
        ats[pl.ds(first, owners)] = out

        def send(n, c2):
            j = first + n

            @pl.when(j != me)
            def _():
                at_copy(j, me).start()
            return c2
        lax.fori_loop(0, owners, send, 0)
        return c

    lax.fori_loop(0, blocks // 4, attend, 0)
    gather_step(2)
    lax.fori_loop(blocks // 4, blocks, attend, 0)
    for n in range(3, len(bits)):
        gather_step(n)
    for load in loads[4:]:
        load.wait()
    atr[me] = ats[me]
    dkf[0:KW] = dk_ref[...].astype(F32)

    ct = ct_ref[...]
    gact_ref[...] = lax.dot_general(
        ct, co_ref[...], (((1,), (1,)), ((), ())), preferred_element_type=F32
    )

    def wait_at(j):
        at_copy(j, j).wait_recv()

    peers(wait_at, S, me)
    for g in range(group):
        for h in range(0, HEADS, 2):
            left = atr[h * group + g]
            right = atr[(h + 1) * group + g]
            if packed:
                left = jnp.concatenate([left[:, :DH], left[:, DH:]], axis=0)
                right = jnp.concatenate([right[:, :DH], right[:, DH:]], axis=0)
            else:
                left, right = left[:, DH:], right[:, DH:]
            att_ref[g * part:(g + 1) * part, h * DH:(h + 2) * DH] = jnp.concatenate(
                [left, right], axis=1
            )
    mid = (
        res_ref[...].astype(F32)
        + jnp.dot(att_ref[...], op_ref[...], preferred_element_type=F32)
    ).astype(BF16)
    mid_ref[...] = mid
    wide = mid.astype(F32)
    centered = wide - jnp.mean(wide, axis=1, keepdims=True)
    rscale = lax.rsqrt(jnp.mean(centered * centered, axis=1, keepdims=True) + EPS)
    gain = ng_ref[...]
    normed = (centered * rscale * gain).astype(BF16)

    gather_step(len(bits))
    if share == 2:
        for r in range(1, S):
            sib_recv(r).wait_recv()

    per = max(1, 256 // cw)
    wide_cols = per * cw

    def weights(n):
        return jnp.concatenate([wf[n * per + i] for i in range(per)], axis=1)

    count = model // wide_cols
    for n in range(count):
        cols = slice(n * wide_cols, (n + 1) * wide_cols)
        value = jnp.dot(normed, weights(n), preferred_element_type=F32)
        gate = sigmoid(jnp.dot(normed, weights(count + n), preferred_element_type=F32))
        val_ref[:, cols] = value
        gate_ref[:, cols] = gate
        gated = (value * gate).astype(BF16)
        gp[16:16 + rows, cols] = gated.astype(F32)
        halo_s[0, :, cols] = gated[:16]
        halo_s[1, :, cols] = gated[rows - 16:]

    def halo(base, act):
        def left_send():
            return rc(halo_s.at[base], halo_r.at[base + 1], h_ss.at[base], h_rs.at[base + 1],
                      lax.rem(me + S - 1, S), dp)

        def right_send():
            return rc(halo_s.at[base + 1], halo_r.at[base], h_ss.at[base + 1], h_rs.at[base],
                      lax.rem(me + 1, S), dp)

        @pl.when(me > 0)
        def _():
            if act == "start":
                left_send().start()
            elif act == "wait":
                rc(halo_s.at[base + 1], halo_r.at[base], h_ss.at[base + 1], h_rs.at[base],
                   lax.rem(me + S - 1, S), dp).wait_recv()
            else:
                left_send().wait_send()

        @pl.when(me < S - 1)
        def _():
            if act == "start":
                right_send().start()
            elif act == "wait":
                rc(halo_s.at[base], halo_r.at[base + 1], h_ss.at[base], h_rs.at[base + 1],
                   lax.rem(me + 1, S), dp).wait_recv()
            else:
                right_send().wait_send()

    def place(base, buf):
        @pl.when(me > 0)
        def _():
            buf[0:16] = halo_r[base].astype(F32)

        @pl.when(me == 0)
        def _():
            buf[0:16] = jnp.zeros((16, model), F32)

        @pl.when(me < S - 1)
        def _():
            buf[16 + rows:32 + rows] = halo_r[base + 1].astype(F32)

        @pl.when(me == S - 1)
        def _():
            buf[16 + rows:32 + rows] = jnp.zeros((16, model), F32)

    halo(0, "start")
    halo(0, "wait")
    place(0, gp)

    LB = 128

    def forward_block(n, c):
        cols = pl.ds(pl.multiple_of(n * LB, LB), LB)
        acc = jnp.zeros((rows, LB), F32)
        for k in range(KW):
            acc = acc + dkf[k:k + 1, cols] * gp[k + 1:k + 1 + rows, cols]
        sg = sigmoid(acc)
        act_ref[:, cols] = (acc * sg).astype(BF16)
        gc = (gact_ref[:, cols] * sg * (1.0 + acc * (1.0 - sg))).astype(BF16)
        cp[16:16 + rows, cols] = gc.astype(F32)
        halo_s[2, :, cols] = gc[:16]
        halo_s[3, :, cols] = gc[rows - 16:]
        return c

    lax.fori_loop(0, model // LB, forward_block, 0)
    halo(2, "start")

    def kernel_block(n, c):
        cols = pl.ds(pl.multiple_of(n * LB, LB), LB)
        gc = cp[16:16 + rows, cols]
        for k in range(KW):
            gkl[k:k + 1, cols] = jnp.sum(
                gp[k + 1:k + 1 + rows, cols] * gc, axis=0, keepdims=True
            )
        gkl[KW:KW + 1, cols] = jnp.zeros((1, LB), F32)
        return c

    lax.fori_loop(0, model // LB, kernel_block, 0)

    kc = gk1s.shape[2]
    across = model // kc
    for j in range(S):
        r0, c0 = (j // across) * 8, (j % across) * kc
        gk1s[j] = gkl[r0:r0 + 8, c0:c0 + kc]

    def k1(j, src):
        return rc(gk1s.at[j], gk1r.at[src], k1_ss.at[j], k1_rs.at[src], j, dp)

    peers(lambda j: k1(j, me).start(), S, me)
    gk1r[me] = gk1s[me]

    lo_ref[...] = (
        mid_ref[...].astype(F32)
        + jnp.dot(act_ref[...], co_ref[...], preferred_element_type=F32)
    ).astype(BF16)
    stores[0].start()

    halo(2, "wait")
    place(2, cp)

    peers(lambda j: k1(j, j).wait_recv(), S, me)
    gk2s[...] = jnp.sum(gk1r[...], axis=0)

    def k2(j, src):
        return rc(gk2s, gk2r.at[src], k2_ss.at[j], k2_rs.at[src], me, j)

    peers(lambda j: k2(j, dp).start(), DPN, dp)
    gk2r[dp] = gk2s[...]

    def backward_block(n, c):
        cols = pl.ds(pl.multiple_of(n * LB, LB), LB)
        acc = jnp.zeros((rows, LB), F32)
        for k in range(KW):
            acc = acc + dkf[k:k + 1, cols] * cp[31 - k:31 - k + rows, cols]
        gate = gate_ref[:, cols]
        first = acc * gate
        gproj_ref[:, cols] = first.astype(BF16)
        gproj_ref[:, pl.ds(pl.multiple_of(model + n * LB, LB), LB)] = (
            first * val_ref[:, cols] * (1.0 - gate)
        ).astype(BF16)
        return c

    lax.fori_loop(0, model // LB, backward_block, 0)

    peers(lambda j: k2(j, j).wait_recv(), DPN, dp)
    gk3r[me] = jnp.sum(gk2r[...], axis=0)

    def k3(j, src):
        return rc(gk3r.at[src], gk3r.at[src], k3_ss.at[j], k3_rs.at[src], j, dp)

    peers(lambda j: k3(j, me).start(), S, me)

    gn = jnp.zeros((rows, model), F32)
    for n in range(2 * count):
        gn = gn + lax.dot_general(
            gproj_ref[:, n * wide_cols:(n + 1) * wide_cols], weights(n),
            (((1,), (1,)), ((), ())), preferred_element_type=F32,
        )
    wide = mid_ref[...].astype(F32)
    centered = wide - jnp.mean(wide, axis=1, keepdims=True)
    rscale = lax.rsqrt(jnp.mean(centered * centered, axis=1, keepdims=True) + EPS)
    hat = centered * rscale
    dh = gn * ng_ref[...]
    inner = (
        dh
        - jnp.mean(dh, axis=1, keepdims=True)
        - hat * jnp.mean(dh * hat, axis=1, keepdims=True)
    )
    gm = (ct_ref[...].astype(F32) + rscale * inner).astype(BF16)
    gm_ref[...] = gm
    stores[1].start()

    att_t = att_ref[...].T
    nc = model // DPN
    orow = go_ref.shape[0]
    for d in range(DPN):
        piece = jnp.dot(att_t, gm[:, d * nc:(d + 1) * nc], preferred_element_type=F32)
        gods[d] = piece.astype(BF16).reshape(S, orow, nc)

    def gd(j, src):
        return rc(gods.at[j], godr.at[src], gd_ss.at[j], gd_rs.at[src], me, j)

    peers(lambda j: gd(j, dp).start(), DPN, dp)
    godr[dp] = gods[dp]
    peers(lambda j: gd(j, j).wait_recv(), DPN, dp)

    def sum_dp(j, c):
        acc = godr[0, j].astype(F32)
        for d in range(1, DPN):
            acc = acc + godr[d, j].astype(F32)
        gos[j] = acc.astype(BF16)
        return c

    lax.fori_loop(0, S, sum_dp, 0)

    def go(j, src):
        return rc(gos.at[j], gor.at[src], g_ss.at[j], g_rs.at[src], j, dp)

    peers(lambda j: go(j, me).start(), S, me)
    gor[me] = gos[me]

    peers(lambda j: k3(j, j).wait_recv(), S, me)
    for j in range(S):
        r0, c0 = (j // across) * 8, (j % across) * kc
        n = min(8, KW - r0)
        gk_ref[r0:r0 + n, c0:c0 + kc] = gk3r[j][:n]

    stores[3].start()

    peers(lambda j: go(j, j).wait_recv(), S, me)
    acc = gor[0].astype(F32)
    for j in range(1, S):
        acc = acc + gor[j].astype(F32)
    gofr[dp] = acc

    def gf(j, src):
        return rc(gofr.at[src], gofr.at[src], gf_ss.at[j], gf_rs.at[src], me, j)

    peers(lambda j: gf(j, dp).start(), DPN, dp)

    def close(j):
        q_copy(j, me).wait_send()
        at_copy(j, me).wait_send()
        k1(j, me).wait_send()
        k3(j, me).wait_send()
        go(j, me).wait_send()

    peers(close, S, me)
    peers(lambda h: kv_copy(h).wait_send(), HEADS, mine)

    def close_hand(i, c):
        src = lax.rem(mine + i, HEADS) * group + member
        for e in range(1, group):
            kv_hand(src, i, e).wait_send()
        return c

    lax.fori_loop(0, HEADS, close_hand, 0)
    for o, order in enumerate(orders):
        for n in range(len(bits)):
            for r in subsets(order, n):
                w_copy(o, r, order[n]).wait_send()
    if share == 2:
        for r in range(1, S):
            sib_copy(r).wait_send()
    halo(0, "close")
    halo(2, "close")

    peers(lambda j: gf(j, j).wait_recv(), DPN, dp)
    for d in range(DPN):
        go_ref[:, d * nc:(d + 1) * nc] = gofr[d]
    stores[2].start()

    def close_dp(j):
        k2(j, dp).wait_send()
        gd(j, dp).wait_send()
        gf(j, dp).wait_send()

    peers(close_dp, DPN, dp)
    for store in stores:
        store.wait()


def hand_on(a, b, c, d, a_out, b_out, c_out, d_out, ab, bb, cb, db, in_sem, out_sem):
    held = [ab, bb, cb, db]
    loads = [
        pltpu.make_async_copy(src, buf, in_sem.at[n])
        for n, (src, buf) in enumerate(zip([a, b, c, d], held))
    ]
    stores = [
        pltpu.make_async_copy(buf, dst, out_sem.at[n])
        for n, (buf, dst) in enumerate(zip(held, [a_out, b_out, c_out, d_out]))
    ]
    for load in loads:
        load.start()
    for load, store in zip(loads, stores):
        load.wait()
        store.start()
    for store in stores:
        store.wait()


def body(queries, keys, values, residual, out_proj, conv_in, conv_out, depth_kernel, norm_gain,
         cotangent):
    S = lax.axis_size("seq")
    DPN = lax.axis_size("dp")
    batch, rows, width = queries.shape
    model = residual.shape[2]
    group = S // HEADS
    part = rows // group
    lane_rows = part // 2 if part % 32 == 0 else part
    cw = conv_in.shape[1]
    kc = 32 * model // (8 * S)
    orow = width // S
    nc = model // DPN
    V = pltpu.VMEM
    D = pltpu.SemaphoreType.DMA
    wide = V((rows, model), F32)
    slim = V((rows, model), BF16)
    scratch = [
        V((rows, width), BF16), V((rows, width), BF16), V((rows, width), BF16), slim,
        V((width, model), BF16), V((model, model), BF16), V((KW, model), BF16),
        V((1, model), F32), slim,
        slim, slim, V((orow, model), F32), V((KW, model), F32),
        D((10,)), D((4,)), D((HEADS, group)),
        V((HEADS, rows, 2 * DH), BF16), V((S, rows, 2 * DH), BF16),
        V((S, lane_rows, 2 * DH), BF16), V((S, lane_rows, 2 * DH), BF16),
        V((S, lane_rows, 2 * DH), BF16), V((S, lane_rows, 2 * DH), BF16),
        V((S, model, cw), BF16),
        V((rows, width), BF16), slim, wide, wide, wide, slim, slim,
        V((rows + 32, model), F32), V((rows + 32, model), F32), V((rows, 2 * model), BF16),
        V((4, 16, model), BF16), V((4, 16, model), BF16), V((32, model), F32),
        V((32, model), F32), V((S, 8, kc), F32), V((S, 8, kc), F32),
        V((8, kc), F32), V((DPN, 8, kc), F32), V((S, 8, kc), F32),
        V((DPN, S, orow, nc), BF16), V((DPN, S, orow, nc), BF16),
        V((S, orow, nc), BF16), V((S, orow, nc), BF16), V((DPN, orow, nc), F32),
        D((HEADS,)), D((S,)), D((S,)), D((S,)), D((S,)), D((S,)), D((8, S)), D((8, S)), D((S,)), D((S,)),
        D((4,)), D((4,)), D((S,)), D((S,)), D((DPN,)), D((DPN,)), D((S,)), D((S,)),
        D((DPN,)), D((DPN,)), D((S,)), D((S,)), D((DPN,)), D((DPN,)),
    ]
    anywhere = pl.BlockSpec(memory_space=pl.ANY)
    shapes = [
        jax.ShapeDtypeStruct((rows, model), BF16),
        jax.ShapeDtypeStruct((rows, model), BF16),
        jax.ShapeDtypeStruct((orow, model), F32),
        jax.ShapeDtypeStruct((KW, model), F32),
    ]
    results = pl.pallas_call(
        functools.partial(kernel, S, DPN),
        out_shape=shapes,
        in_specs=[anywhere] * 10,
        out_specs=[anywhere] * 4,
        scratch_shapes=scratch,
        compiler_params=pltpu.CompilerParams(
            collective_id=0, has_side_effects=True, vmem_limit_bytes=60 * 1024 * 1024
        ),
    )(
        queries[0], keys[0], values[0], residual[0], out_proj, conv_in, conv_out, depth_kernel,
        norm_gain.reshape(1, model), cotangent[0],
    )
    lo, gm, go, gk = pl.pallas_call(
        hand_on,
        out_shape=shapes,
        in_specs=[anywhere] * 4,
        out_specs=[anywhere] * 4,
        scratch_shapes=[V(x.shape, x.dtype) for x in shapes] + [D((4,)), D((4,))],
    )(*results)
    return lo[None], gm[None], go, gk


def solution(mesh):
    return jax.shard_map(
        body,
        mesh=mesh,
        in_specs=(
            P("dp", "seq", None),
            P("dp", "seq", None),
            P("dp", "seq", None),
            P("dp", "seq", None),
            P(),
            P(None, "seq"),
            P(),
            P(),
            P(),
            P("dp", "seq", None),
        ),
        out_specs=(P("dp", "seq", None), P("dp", "seq", None), P("seq", None), P()),
        check_vma=False,
    )
```
